32 devices in a mesh: groups: 2 (over y), bundle: 16 (over z, x, core).
Axes of the slice: x: 2, y: 2, z: 4, core: 2. Of those that a mesh axis runs over, the one named last changes fastest.
Arguments:
- objective: float32 [512, 8192], P(('groups', 'bundle')), parts along dimension 0, may hold values from -8 to 8
- demands: float32 [512, 8192], P(('groups', 'bundle')), parts along dimension 0, may hold values from -6 to 6
- multipliers: float32 [512, 6144], P(('groups', 'bundle')), parts along dimension 0, may hold values from -4 to 4
- probability: float32 [512], P(('groups', 'bundle')), parts along dimension 0, may hold values from 1 to 9
- matrix_tiles: bfloat16 [512, 128, 128], P('groups'), parts along dimension 0, may hold values from -0.25 to 0.25
- tile_row: int32 [512], P('groups'), parts along dimension 0, may hold values from 0 to 63, as said below
- tile_col: int32 [512], P('groups'), parts along dimension 0, may hold values from 0 to 63
- unit_kind: int32 [16384], P('groups'), parts along dimension 0, may hold values 0 or 1
- leaf_node: int32 [512], P(('groups', 'bundle')), parts along dimension 0, may hold values from 0 to 63, as said below
- node_parent: int32 [128], P('groups'), parts along dimension 0, may hold values from 0 to 7, as said below
Outputs:
- solution: float32 [512, 8192], P(('groups', 'bundle')), parts along dimension 0
- new_multipliers: float32 [512, 6144], P(('groups', 'bundle')), parts along dimension 0
- hedging_gap: float32 [4], P('groups'), parts along dimension 0
- lagrange_bound: float32 [4], P('groups'), parts along dimension 0
The draws below stay inside these ranges and needn't reach their ends.
There are 2 independent parts, one for each index of `groups`. The reference program is written for one: setup_inputs(seed, part) draws one part's arguments, and reference() takes and returns one part's arrays. A program takes and returns all parts, laid end to end along the dimension named above; each array names one. Nothing has to cross between parts.
Inputs may be any that keep to these rules, and one draw needn't show every extreme that they name: `leaf_node`: each of the 64 third-section nodes holds exactly 4 scenarios. `node_parent`: each second-section node is the parent of exactly 8 third-section nodes. `tile_row`: each tile row holds exactly 4 tiles.
All inputs are finite; a program needn't handle non-finite values.
Results may differ from the reference program's by a relative error of at most 0.0011.
Values sent between devices are 32-bit elements; how exact they have to be, the bound alone decides.
A program may use at most 128 MiB of HBM per device.

```python
import jax
import jax.numpy as jnp
from jax import lax

SECTION_VARS = 2048
TILE = 128
TILES_ROW = 4
NODES2 = 8
NODES3 = 64
ITERS = 2
PDHG_STEPS = 2
SCEN = 256
NV = 8192
VAR_BLOCKS = 64
CON_BLOCKS = 64
NC = 8192
NTILES = 256


def draw_probability(key, part):
    key = jax.random.fold_in(key, 11)
    ramp = jnp.arange(SCEN, dtype=jnp.float32) / max(SCEN - 1, 1)
    factor = jnp.exp(jax.random.uniform(key, (SCEN,), jnp.float32, 0.0, jnp.log(3.0)))
    return ((1.0 + 2.0 * ramp) * factor).astype(jnp.float32)


def draw_leaf_node(key, part):
    key = jax.random.fold_in(key, 12)
    order = jax.random.permutation(key, SCEN)
    return (order % NODES3).astype(jnp.int32)


def draw_node_parent(key, part):
    key = jax.random.fold_in(key, 13)
    order = jax.random.permutation(key, NODES3)
    return (order % NODES2).astype(jnp.int32)


def draw_tile_row(key, part):
    key = jax.random.fold_in(key, 14)
    order = jax.random.permutation(key, NTILES)
    return (order % CON_BLOCKS).astype(jnp.int32)


def place_ends(array, rng, least, largest):
    longest = array.shape.index(max(array.shape))
    spots = []
    for shift in (0, 1):
        where = [jax.random.randint(jax.random.fold_in(rng, axis), (), 0, length) for axis, length in enumerate(array.shape)]
        where[longest] = (where[longest] + shift) % array.shape[longest]
        spots.append(tuple(where))
    return array.at[spots[0]].set(least).at[spots[1]].set(largest)


def shard_levels(key, dims, shards, low, largest):
    gain, own = 1.0, jax.random.fold_in(key, 6)
    for axis_at, parts in shards:
        heights = jnp.exp(jax.random.uniform(jax.random.fold_in(own, axis_at), (parts,), jnp.float32, low / len(shards), largest / len(shards)))
        gain = gain * jnp.repeat(heights, dims[axis_at] // parts).reshape([-1 if axis == axis_at else 1 for axis in range(len(dims))])
    return gain


def gaussian(stream_key, dims, scale, most, pieces=(), kind=jnp.bfloat16):
    drawn = scale * jax.random.normal(stream_key, dims, jnp.float32)
    if pieces:
        drawn = drawn * shard_levels(stream_key, dims, pieces, -0.22, 0.18)
    return jnp.clip(drawn, -most, most).astype(kind)


def setup_inputs(seed: int = 0, part: int = 0) -> dict:
    splits = jax.random.split(jax.random.key(seed), 11)
    own_keys = jax.random.split(jax.random.fold_in(splits[10], part), 11)
    objective = gaussian(own_keys[0], (SCEN, NV), 2.0, 8.0, ((0, 16),), jnp.float32)
    demands = gaussian(own_keys[1], (SCEN, NC), 1.0, 6.0, ((0, 16),), jnp.float32)
    multipliers = gaussian(own_keys[2], (SCEN, 3 * SECTION_VARS), 0.5, 4.0, ((0, 16),), jnp.float32)
    probability = draw_probability(jax.random.fold_in(jax.random.fold_in(splits[10], part), 71), part)
    matrix_tiles = gaussian(own_keys[4], (NTILES, TILE, TILE), (TILES_ROW * TILE) ** -0.5, 0.25)
    tile_row = draw_tile_row(jax.random.fold_in(jax.random.fold_in(splits[10], part), 71), part)
    tile_col = place_ends(jax.random.randint(own_keys[6], (NTILES,), 0, VAR_BLOCKS), jax.random.fold_in(own_keys[6], 1), 0, VAR_BLOCKS - 1).astype(jnp.int32)
    unit_kind = place_ends((jax.random.randint(own_keys[7], (NV,), 0, 2) < 1).astype(jnp.int32), jax.random.fold_in(own_keys[7], 1), 0, 1)
    leaf_node = draw_leaf_node(jax.random.fold_in(jax.random.fold_in(splits[10], part), 71), part)
    node_parent = draw_node_parent(jax.random.fold_in(jax.random.fold_in(splits[10], part), 71), part)
    return dict(objective=objective, demands=demands, multipliers=multipliers, probability=probability, matrix_tiles=matrix_tiles, tile_row=tile_row, tile_col=tile_col, unit_kind=unit_kind, leaf_node=leaf_node, node_parent=node_parent)


step_tau = 0.4
step_sigma = 0.4
penalty = 0.5


def forward(matrix_tiles, tile_row, tile_col, vector, con_blocks):
    batch_size = vector.shape[0]
    tile_size = matrix_tiles.shape[1]
    blocks = vector.astype(jnp.float32).reshape(batch_size, -1, tile_size)
    picked = blocks[:, tile_col, :]
    product = jnp.einsum("tij,stj->sti", matrix_tiles.astype(jnp.float32), picked, precision=lax.Precision.HIGHEST)
    summed = jax.ops.segment_sum(jnp.moveaxis(product, 1, 0), tile_row, num_segments=con_blocks)
    return jnp.moveaxis(summed, 0, 1).reshape(batch_size, -1)


def backward(matrix_tiles, tile_row, tile_col, vector, var_blocks):
    batch_size = vector.shape[0]
    tile_size = matrix_tiles.shape[1]
    blocks = vector.astype(jnp.float32).reshape(batch_size, -1, tile_size)
    picked = blocks[:, tile_row, :]
    product = jnp.einsum("tij,sti->stj", matrix_tiles.astype(jnp.float32), picked, precision=lax.Precision.HIGHEST)
    summed = jax.ops.segment_sum(jnp.moveaxis(product, 1, 0), tile_col, num_segments=var_blocks)
    return jnp.moveaxis(summed, 0, 1).reshape(batch_size, -1)


def reference(objective, demands, multipliers, probability, matrix_tiles, tile_row, tile_col, unit_kind, leaf_node, node_parent):
    section_width = multipliers.shape[1] // 3
    tile_size = matrix_tiles.shape[1]
    var_blocks = objective.shape[1] // tile_size
    con_blocks = demands.shape[1] // tile_size
    upper = jnp.where(unit_kind == 1, 1.0, 3.0).astype(jnp.float32)
    leaf_two = node_parent[leaf_node].astype(jnp.int32)
    leaf_one = jnp.zeros_like(leaf_node)
    groupings = ((leaf_one, 1), (leaf_two, NODES2), (leaf_node, NODES3))
    total_prob = jnp.sum(probability)
    zeros_section = jnp.zeros((objective.shape[0], section_width), jnp.float32)

    def consensus(values):
        result = []
        for section_index in range(3):
            labels, node_count = groupings[section_index]
            part_values = values[:, section_index * section_width:(section_index + 1) * section_width]
            sums = jax.ops.segment_sum(probability[:, None] * part_values, labels, num_segments=node_count)
            totals = jax.ops.segment_sum(probability, labels, num_segments=node_count)
            result.append((sums / totals[:, None])[labels])
        return jnp.concatenate(result, axis=1)

    def primal_dual(primal, dual, linear, anchor):
        gradient = linear + backward(matrix_tiles, tile_row, tile_col, dual.astype(jnp.bfloat16), var_blocks)
        if anchor is not None:
            gradient = gradient + penalty * jnp.concatenate([primal[:, :3 * section_width] - anchor, zeros_section], axis=1)
        moved = jnp.clip(primal - step_tau * gradient, 0.0, upper)
        image = forward(matrix_tiles, tile_row, tile_col, (2.0 * moved - primal).astype(jnp.bfloat16), con_blocks)
        return moved, jnp.maximum(dual + step_sigma * (image - demands), 0.0)

    primal = jnp.zeros_like(objective)
    dual = jnp.zeros_like(demands)
    spoke_primal = jnp.zeros_like(objective)
    spoke_dual = jnp.zeros_like(demands)
    weights_now = multipliers
    anchor = None
    gap_terms = []
    bound_terms = []
    for iteration in range(ITERS):
        linear = objective + jnp.concatenate([weights_now, zeros_section], axis=1)
        for inner in range(PDHG_STEPS):
            primal, dual = primal_dual(primal, dual, linear, anchor)
        agreed = consensus(primal)
        deviation = primal[:, :3 * section_width] - agreed
        gap_terms.append(jnp.sum(probability * jnp.sum(deviation * deviation, axis=1)))
        for inner in range(PDHG_STEPS):
            spoke_primal, spoke_dual = primal_dual(spoke_primal, spoke_dual, linear, None)
        reduced = linear + backward(matrix_tiles, tile_row, tile_col, spoke_dual.astype(jnp.bfloat16), var_blocks)
        bound_terms.append(jnp.sum(probability * (jnp.sum(reduced * spoke_primal, axis=1) - jnp.sum(demands * spoke_dual, axis=1))))
        weights_now = weights_now + penalty * deviation
        anchor = agreed
    hedging_gap = jnp.stack(gap_terms) / (3 * section_width * total_prob)
    lagrange_bound = jnp.stack(bound_terms) / (objective.shape[1] * total_prob)
    return primal, weights_now, hedging_gap, lagrange_bound
```

```python
import functools

import jax
import jax.numpy as jnp
from jax import lax
from jax.experimental import pallas as pl
from jax.experimental.pallas import tpu as pltpu
from jax.sharding import PartitionSpec as P

NODES2 = 8
ITERS = 2
PDHG_STEPS = 2


step_tau = 0.4
step_sigma = 0.4
penalty = 0.5


def forward(grouped_tiles, sorted_cols, vector):
    batch_size = vector.shape[0]
    con_blocks, per_row, tile_size = (
        grouped_tiles.shape[0],
        grouped_tiles.shape[1],
        grouped_tiles.shape[2],
    )
    blocks = vector.reshape(batch_size, -1, tile_size)
    picked = jnp.take(blocks, sorted_cols, axis=1).reshape(
        batch_size, con_blocks, per_row, tile_size
    )
    product = jnp.einsum(
        "rkij,srkj->sri", grouped_tiles, picked, preferred_element_type=jnp.float32
    )
    return product.reshape(batch_size, -1)


def backward(grouped_tiles, cols_onehot, vector):
    batch_size = vector.shape[0]
    con_blocks, per_row, tile_size = (
        grouped_tiles.shape[0],
        grouped_tiles.shape[1],
        grouped_tiles.shape[2],
    )
    blocks = vector.reshape(batch_size, con_blocks, tile_size)
    product = jnp.einsum(
        "rkij,sri->srkj", grouped_tiles, blocks, preferred_element_type=jnp.float32
    )
    product = product.reshape(batch_size, con_blocks * per_row, tile_size)
    summed = jnp.einsum("vt,stj->svj", cols_onehot, product, precision=lax.Precision.HIGH)
    return summed.reshape(batch_size, -1)


def general(
    objective,
    demands,
    multipliers,
    probability,
    matrix_tiles,
    tile_row,
    tile_col,
    unit_kind,
    leaf_node,
    node_parent,
):
    scen_count = objective.shape[0]
    section_width = multipliers.shape[1] // 3
    tile_size = matrix_tiles.shape[1]
    var_blocks = objective.shape[1] // tile_size
    con_blocks = demands.shape[1] // tile_size
    tile_order = jnp.argsort(tile_row, stable=True)
    grouped_tiles = jnp.take(matrix_tiles, tile_order, axis=0).reshape(
        con_blocks, -1, tile_size, tile_size
    )
    sorted_cols = jnp.take(tile_col, tile_order)
    cols_onehot = (sorted_cols[None, :] == jnp.arange(var_blocks, dtype=jnp.int32)[:, None]).astype(
        jnp.float32
    )
    upper = jnp.where(unit_kind == 1, 1.0, 3.0).astype(jnp.float32)
    member_three = (
        leaf_node[:, None] == jnp.arange(node_parent.shape[0], dtype=jnp.int32)[None, :]
    ).astype(jnp.float32)
    parent_map = (node_parent[:, None] == jnp.arange(NODES2, dtype=jnp.int32)[None, :]).astype(
        jnp.float32
    )
    member_two = jnp.dot(member_three, parent_map, precision=lax.Precision.HIGHEST)
    member_one = jnp.ones((scen_count, 1), jnp.float32)
    members = (member_one, member_two, member_three)
    local_weights = jnp.concatenate(
        [jnp.dot(probability, member, precision=lax.Precision.HIGHEST) for member in members]
    )
    node_totals = lax.psum(local_weights, "bundle")
    total_prob = node_totals[0]
    weight_flat = jnp.repeat(node_totals, section_width)
    zeros_section = jnp.zeros((scen_count, section_width), jnp.float32)

    def primal_dual(primal, dual, linear, anchor, dual_back):
        if dual_back is None:
            dual_back = backward(grouped_tiles, cols_onehot, dual.astype(jnp.bfloat16))
        gradient = linear + dual_back
        if anchor is not None:
            gradient = gradient + penalty * jnp.concatenate(
                [primal[:, : 3 * section_width] - anchor, zeros_section], axis=1
            )
        moved = jnp.clip(primal - step_tau * gradient, 0.0, upper)
        image = forward(grouped_tiles, sorted_cols, (2.0 * moved - primal).astype(jnp.bfloat16))
        return (moved, jnp.maximum(dual + step_sigma * (image - demands), 0.0))

    primal = jnp.zeros_like(objective)
    dual = jnp.zeros_like(demands)
    spoke_primal = primal
    spoke_dual = dual
    weights_now = multipliers
    anchor = None
    hub_back = None
    spoke_back = None
    gap_terms = []
    bound_terms = []
    for iteration in range(ITERS):
        linear = objective + jnp.concatenate([weights_now, zeros_section], axis=1)
        for inner in range(PDHG_STEPS):
            primal, dual = primal_dual(
                primal, dual, linear, anchor, hub_back if inner == 0 else None
            )
        hub_back = None
        pieces = []
        for section_index in range(3):
            consensus_member = members[section_index]
            part_values = primal[
                :, section_index * section_width : (section_index + 1) * section_width
            ]
            weighted = consensus_member * probability[:, None]
            pieces.append(
                jnp.dot(weighted.T, part_values, precision=lax.Precision.HIGHEST).reshape(-1)
            )
        flat_sums = jnp.concatenate(pieces)
        mean_values = lax.psum(flat_sums, "bundle") / weight_flat
        result = []
        offset = 0
        for consensus_member in members:
            node_count = consensus_member.shape[1]
            node_table = mean_values[offset : offset + node_count * section_width].reshape(
                node_count, section_width
            )
            result.append(jnp.dot(consensus_member, node_table, precision=lax.Precision.HIGHEST))
            offset = offset + node_count * section_width
        agreed = jnp.concatenate(result, axis=1)
        deviation = primal[:, : 3 * section_width] - agreed
        gap_term = jnp.sum(probability * jnp.sum(deviation * deviation, axis=1))
        if iteration == 0:
            spoke_primal, spoke_dual = (primal, dual)
        else:
            for inner in range(PDHG_STEPS):
                spoke_primal, spoke_dual = primal_dual(
                    spoke_primal, spoke_dual, linear, None, spoke_back if inner == 0 else None
                )
        spoke_back = backward(grouped_tiles, cols_onehot, spoke_dual.astype(jnp.bfloat16))
        if iteration == 0:
            hub_back = spoke_back
        reduced = linear + spoke_back
        bound_term = jnp.sum(
            probability
            * (jnp.sum(reduced * spoke_primal, axis=1) - jnp.sum(demands * spoke_dual, axis=1))
        )
        gap_terms.append(lax.psum(gap_term, "bundle"))
        bound_terms.append(lax.psum(bound_term, "bundle"))
        weights_now = weights_now + penalty * deviation
        anchor = agreed
    gap_totals = jnp.stack(gap_terms)
    bound_totals = jnp.stack(bound_terms)
    hedging_gap = gap_totals / (3 * section_width * total_prob)
    lagrange_bound = bound_totals / (objective.shape[1] * total_prob)
    return (primal, weights_now, hedging_gap, lagrange_bound)


MESH = pl.DeviceIdType.MESH
ROW_TILE, ROW_COL, COL_TILE, COL_ROW, COL_KEEP, COL_LAST = range(6)
HIGHEST = lax.Precision.HIGHEST


def tables(tile_row, tile_col, var_blocks):
    count = tile_row.shape[0]
    place = jnp.arange(count, dtype=jnp.int32)
    keys = jnp.stack([tile_row, tile_col]) * count + place
    rank = jnp.sum((keys[:, None, :] < keys[:, :, None]).astype(jnp.int32), axis=2)
    code = place + count * (tile_row + 256 * tile_col)
    hit = rank[:, :, None] == place[None, None, :]
    packed = jnp.sum(jnp.where(hit, code[None, :, None], 0), axis=1)
    tile = packed % count
    row = (packed // count) % 256
    col = packed // (count * 256)
    keep = jnp.concatenate([jnp.zeros(1, jnp.int32), (col[1, 1:] == col[1, :-1]).astype(jnp.int32)])
    block = jnp.arange(count, dtype=jnp.int32)
    upto = jnp.sum((tile_col[None, :] <= block[:, None]).astype(jnp.int32), axis=1)
    own = jnp.any(tile_col[None, :] == block[:, None], axis=1)
    last = jnp.where(own, upto - 1, count)
    return jnp.concatenate([tile[0], col[0], tile[1], row[1], keep, last])


def mega(
    parts,
    idx_ref,
    objective_ref,
    demands_ref,
    mult_ref,
    kind_ref,
    meta_ref,
    tiles_hbm,
    x_out,
    w_out,
    scalars_out,
    tiles,
    x,
    y,
    xs,
    ys,
    q,
    h,
    a,
    h2,
    a2,
    runs,
    runs2,
    meta_all,
    mask2,
    mask3,
    put1,
    got1,
    put2,
    got2,
    back1,
    ret1,
    back2,
    ret2,
    tile_sem,
    meta_send,
    meta_recv,
    put_send,
    put_recv,
    ret_send,
    ret_recv,
):
    me = lax.axis_index("bundle")
    blocks = x.shape[0]
    rows = x.shape[1]
    count = tiles.shape[0]
    con_blocks = y.shape[0]
    per_row = count // con_blocks
    free = blocks - 3 * parts

    tile_copy = pltpu.make_async_copy(tiles_hbm, tiles, tile_sem)
    tile_copy.start()

    barrier = pltpu.get_barrier_semaphore()

    def greet(k, carry):
        pl.semaphore_signal(
            barrier, inc=1, device_id={"bundle": lax.rem(me + k, parts)}, device_id_type=MESH
        )
        return carry

    lax.fori_loop(1, parts, greet, 0)

    def lanes(block):
        return pl.ds(pl.multiple_of(block * 128, 128), 128)

    def upper(block):
        return jnp.where(kind_ref[:, lanes(block)] == 1, 1.0, 3.0).astype(jnp.float32)

    def index(table, item):
        return idx_ref[table * count + item]

    def first(block, with_w):
        linear = objective_ref[:, lanes(block)]
        if with_w:
            linear = linear + mult_ref[:, lanes(block)]
        q[block] = linear
        moved = jnp.clip(-step_tau * linear, 0.0, upper(block))
        x[block] = moved
        h[block] = (2.0 * moved).astype(jnp.bfloat16)

    def loop(start, stop, width, body):
        def many(i, carry):
            for u in range(width):
                body(start + i * width + u)
            return carry

        lax.fori_loop(0, (stop - start) // width, many, 0)

    loop(0, 3 * parts, 4, lambda block: first(block, True))
    loop(3 * parts, blocks, 4, lambda block: first(block, False))

    pl.semaphore_wait(barrier, parts - 1)

    def meta_copy(k):
        return pltpu.make_async_remote_copy(
            src_ref=meta_ref,
            dst_ref=meta_all.at[me],
            send_sem=meta_send.at[k],
            recv_sem=meta_recv.at[k],
            device_id={"bundle": lax.rem(me + k, parts)},
            device_id_type=MESH,
        )

    def put_copy(k, put, got, turn):
        peer = lax.rem(me + k, parts)
        return pltpu.make_async_remote_copy(
            src_ref=put.at[peer],
            dst_ref=got.at[me],
            send_sem=put_send.at[turn, k],
            recv_sem=put_recv.at[turn, k],
            device_id={"bundle": peer},
            device_id_type=MESH,
        )

    def ret_copy(k, back, ret, turn):
        peer = lax.rem(me + k, parts)
        return pltpu.make_async_remote_copy(
            src_ref=back.at[peer],
            dst_ref=ret.at[me],
            send_sem=ret_send.at[turn, k],
            recv_sem=ret_recv.at[turn, k],
            device_id={"bundle": peer},
            device_id_type=MESH,
        )

    def each(body):
        def step(k, carry):
            body(k)
            return carry

        lax.fori_loop(1, parts, step, 0)

    each(lambda k: meta_copy(k).start())
    meta_all[me] = meta_ref[...]

    def forward(vec, done):
        def row(r):
            picked = [vec[index(ROW_COL, r * per_row + k)] for k in range(per_row)]
            mats = [tiles[index(ROW_TILE, r * per_row + k)] for k in range(per_row)]
            image = lax.dot_general(
                jnp.concatenate(picked, axis=1),
                jnp.concatenate(mats, axis=1),
                (((1,), (1,)), ((), ())),
                preferred_element_type=jnp.float32,
            )
            done(r, image)

        loop(0, con_blocks, 4, row)

    def backward(vec, into):
        into[count] = jnp.zeros(into.shape[1:], jnp.float32)

        def many(i, total):
            for u in range(8):
                t = i * 8 + u
                product = jnp.dot(
                    vec[index(COL_ROW, t)],
                    tiles[index(COL_TILE, t)],
                    preferred_element_type=jnp.float32,
                )
                total = jnp.where(index(COL_KEEP, t) == 1, total, 0.0) + product
                into[t] = total
            return total

        lax.fori_loop(0, count // 8, many, jnp.zeros(into.shape[1:], jnp.float32))

    tile_copy.wait()

    def dual_first(r, image):
        new = jnp.maximum(step_sigma * (image - demands_ref[:, lanes(r)]), 0.0)
        y[r] = new
        a[r] = new.astype(jnp.bfloat16)

    forward(h, dual_first)
    backward(a, runs)

    def second(block):
        old = x[block]
        gradient = q[block] + runs[index(COL_LAST, block)]
        moved = jnp.clip(old - step_tau * gradient, 0.0, upper(block))
        x[block] = moved
        h[block] = (2.0 * moved - old).astype(jnp.bfloat16)
        return moved

    def scatter(update, put, got, turn):
        def column(owner):
            for section in range(3):
                put[owner, section * rows : (section + 1) * rows, :] = update(
                    section * parts + owner
                )

        def send(k):
            column(lax.rem(me + k, parts))
            put_copy(k, put, got, turn).start()

        each(send)
        column(me)
        got[me] = put[me]

    scatter(second, put1, got1, 0)
    loop(3 * parts, blocks, 4, second)

    each(lambda k: meta_copy(k).wait_recv())
    table = meta_all[...].reshape(parts * rows, 128)
    across = table.T
    leaf_col, p_col, two_col = table[:, 0:1], table[:, 1:2], table[:, 2:3]
    leaf_row, p_row, two_row = across[0:1, :], across[1:2, :], across[2:3, :]
    mask3[...] = jnp.where(leaf_col == leaf_row, p_row, 0.0)
    mask2[...] = jnp.where(two_col == two_row, p_row, 0.0)

    def dual_second(r, image):
        new = jnp.maximum(y[r] + step_sigma * (image - demands_ref[:, lanes(r)]), 0.0)
        y[r] = new
        a[r] = new.astype(jnp.bfloat16)

    forward(h, dual_second)
    backward(a, runs)

    my_p = meta_ref[:, 1:2]

    def bound(primal, dual, carry_runs):
        def body(i, total):
            for u in range(4):
                block = i * 4 + u
                total = total + (
                    (q[block] + carry_runs[index(COL_LAST, block)]) * primal(block)
                    - demands_ref[:, lanes(block)] * dual(block)
                )
            return total

        total = lax.fori_loop(0, blocks // 4, body, jnp.zeros((rows, 128), jnp.float32))
        return jnp.sum(my_p * total, axis=0, keepdims=True)

    bound_first = bound(lambda block: x[block], lambda block: y[block], runs)

    def consensus(put, got, back, ret, bound_row, turn):
        each(lambda k: put_copy(k, put, got, turn).wait_recv())
        everyone = meta_all[...].reshape(parts * rows, 128)
        prob = everyone[:, 1:2]
        one, two, three = [
            got[:, section * rows : (section + 1) * rows, :].reshape(parts * rows, 128)
            for section in range(3)
        ]
        weights3, weights2 = mask3[...], mask2[...]
        mean3 = jnp.dot(weights3, three, precision=HIGHEST) / jnp.sum(
            weights3, axis=1, keepdims=True
        )
        mean2 = jnp.dot(weights2, two, precision=HIGHEST) / jnp.sum(
            weights2, axis=1, keepdims=True
        )
        mean1 = jnp.sum(prob * one, axis=0, keepdims=True) / jnp.sum(prob, keepdims=True)
        square = (three - mean3) ** 2 + (two - mean2) ** 2 + (one - mean1) ** 2
        gap_row = jnp.sum(prob * square, axis=0, keepdims=True)
        back[:, 0:rows, :] = mean3.reshape(parts, rows, 128)
        back[:, rows : 2 * rows, :] = mean2.reshape(parts, rows, 128)
        line = lax.broadcasted_iota(jnp.int32, (8, 128), 0)
        extra = jnp.where(
            line == 0, mean1, jnp.where(line == 1, gap_row, jnp.where(line == 2, bound_row, 0.0))
        )
        back[:, 2 * rows :, :] = jnp.broadcast_to(extra[None], (parts, 8, 128))
        each(lambda k: ret_copy(k, back, ret, turn).start())
        ret[me] = back[me]
        each(lambda k: ret_copy(k, back, ret, turn).wait_recv())

    def drain(put, got, back, ret, turn):
        each(lambda k: put_copy(k, put, got, turn).wait_send())
        each(lambda k: ret_copy(k, back, ret, turn).wait_send())

    def agreed(ret, section, owner):
        if section == 0:
            return ret[owner, 2 * rows : 2 * rows + 1, :]
        if section == 1:
            return ret[owner, rows : 2 * rows, :]
        return ret[owner, 0:rows, :]

    consensus(put1, got1, back1, ret1, bound_first, 0)

    def third(block, section, owner):
        old = x[block]
        linear = q[block]
        carry = runs[index(COL_LAST, block)]
        limit = upper(block)
        if section is None:
            moved = jnp.clip(old - step_tau * (linear + carry), 0.0, limit)
            spoke = moved
        else:
            mean = agreed(ret1, section, owner)
            half = penalty * (old - mean)
            w = mult_ref[:, lanes(block)] + half
            w_out[:, lanes(block)] = w
            linear = objective_ref[:, lanes(block)] + w
            q[block] = linear
            gradient = linear + carry
            moved = jnp.clip(old - step_tau * (gradient + half), 0.0, limit)
            spoke = jnp.clip(old - step_tau * gradient, 0.0, limit)
        x[block] = moved
        xs[block] = spoke
        h2[block] = jnp.concatenate(
            [2.0 * moved - old, 2.0 * spoke - old], axis=0
        ).astype(jnp.bfloat16)

    def sections(body):
        def step(owner):
            for section in range(3):
                body(section * parts + owner, section, owner)

        loop(0, parts, 2, step)

    sections(third)
    loop(3 * parts, blocks, 4, lambda block: third(block, None, None))

    def dual_third(r, image):
        old = y[r]
        right = demands_ref[:, lanes(r)]
        hub = jnp.maximum(old + step_sigma * (image[0:rows] - right), 0.0)
        spoke = jnp.maximum(old + step_sigma * (image[rows:] - right), 0.0)
        ys[r] = spoke
        a2[r] = jnp.concatenate([hub, spoke], axis=0).astype(jnp.bfloat16)

    forward(h2, dual_third)
    backward(a2, runs2)

    def fourth(block, section, owner):
        both = runs2[index(COL_LAST, block)]
        linear = q[block]
        limit = upper(block)
        old = x[block]
        gradient = linear + both[0:rows]
        if section is not None:
            gradient = gradient + penalty * (old - agreed(ret1, section, owner))
        moved = jnp.clip(old - step_tau * gradient, 0.0, limit)
        x_out[:, lanes(block)] = moved
        old_spoke = xs[block]
        spoke = jnp.clip(old_spoke - step_tau * (linear + both[rows:]), 0.0, limit)
        xs[block] = spoke
        h[block] = (2.0 * spoke - old_spoke).astype(jnp.bfloat16)
        return moved

    each(lambda k: meta_copy(k).wait_send())
    drain(put1, got1, back1, ret1, 0)

    def scatter_last():
        def column(owner):
            for section in range(3):
                put2[owner, section * rows : (section + 1) * rows, :] = fourth(
                    section * parts + owner, section, owner
                )

        def send(k):
            column(lax.rem(me + k, parts))
            put_copy(k, put2, got2, 1).start()

        each(send)
        column(me)
        got2[me] = put2[me]

    scatter_last()
    loop(3 * parts, blocks, 4, lambda block: fourth(block, None, None))

    def dual_fourth(r, image):
        new = jnp.maximum(ys[r] + step_sigma * (image - demands_ref[:, lanes(r)]), 0.0)
        ys[r] = new
        a[r] = new.astype(jnp.bfloat16)

    forward(h, dual_fourth)
    backward(a, runs)
    bound_second = bound(lambda block: xs[block], lambda block: ys[block], runs)
    consensus(put2, got2, back2, ret2, bound_second, 1)

    def finish(block, section, owner):
        w_out[:, lanes(block)] = w_out[:, lanes(block)] + penalty * (
            x_out[:, lanes(block)] - agreed(ret2, section, owner)
        )

    sections(finish)
    drain(put2, got2, back2, ret2, 1)
    total = jnp.sum(meta_all[...].reshape(parts * rows, 128)[:, 1:2])
    gap_scale = 1.0 / (3 * parts * 128 * total)
    bound_scale = 1.0 / (blocks * 128 * total)
    for iteration, ret in enumerate((ret1, ret2)):
        scalars_out[iteration] = jnp.sum(ret[:, 2 * rows + 1 : 2 * rows + 2, :]) * gap_scale
        scalars_out[2 + iteration] = jnp.sum(ret[:, 2 * rows + 2 : 2 * rows + 3, :]) * bound_scale


def shards(
    parts,
    objective,
    demands,
    multipliers,
    probability,
    matrix_tiles,
    tile_row,
    tile_col,
    unit_kind,
    leaf_node,
    node_parent,
):
    rows, width = objective.shape
    tile = matrix_tiles.shape[1]
    section = multipliers.shape[1] // 3
    count = matrix_tiles.shape[0]
    fits = (
        tile == 128
        and rows == 16
        and section == parts * tile
        and width == demands.shape[1]
        and width // tile <= min(count, 256)
        and parts > 1
    )
    if not fits:
        return general(
            objective,
            demands,
            multipliers,
            probability,
            matrix_tiles,
            tile_row,
            tile_col,
            unit_kind,
            leaf_node,
            node_parent,
        )
    blocks = width // tile
    table = tables(tile_row, tile_col, blocks)
    nodes = jnp.arange(node_parent.shape[0], dtype=jnp.int32)
    parent = jnp.sum(
        jnp.where(leaf_node[:, None] == nodes[None, :], node_parent[None, :], 0), axis=1
    )
    lane = jnp.arange(tile)[None, :]
    meta = jnp.where(
        lane == 0,
        leaf_node[:, None].astype(jnp.float32),
        jnp.where(
            lane == 1,
            probability[:, None],
            jnp.where(lane == 2, parent[:, None].astype(jnp.float32), 0.0),
        ),
    )
    f32, bf16 = jnp.float32, jnp.bfloat16
    state = pltpu.VMEM((blocks, rows, tile), f32)
    vec = pltpu.VMEM((blocks, rows, tile), bf16)
    vec2 = pltpu.VMEM((blocks, 2 * rows, tile), bf16)
    put = pltpu.VMEM((parts, 3 * rows, tile), f32)
    ret = pltpu.VMEM((parts, 2 * rows + 8, tile), f32)
    mask = pltpu.VMEM((parts * rows, parts * rows), f32)
    sems = pltpu.SemaphoreType.DMA((2, parts))
    vmem = pl.BlockSpec(memory_space=pltpu.VMEM)
    smem = pl.BlockSpec(memory_space=pltpu.SMEM)
    flops = 2 * count * tile * tile * rows * 10
    solution_x, new_w, scalars = pl.pallas_call(
        functools.partial(mega, parts),
        out_shape=(
            jax.ShapeDtypeStruct((rows, width), f32),
            jax.ShapeDtypeStruct(multipliers.shape, f32),
            jax.ShapeDtypeStruct((4,), f32),
        ),
        in_specs=[smem, vmem, vmem, vmem, vmem, vmem, pl.BlockSpec(memory_space=pl.ANY)],
        out_specs=(vmem, vmem, smem),
        scratch_shapes=[
            pltpu.VMEM(matrix_tiles.shape, bf16),
            state,
            state,
            state,
            state,
            state,
            vec,
            vec,
            vec2,
            vec2,
            pltpu.VMEM((count + 1, rows, tile), f32),
            pltpu.VMEM((count + 1, 2 * rows, tile), f32),
            pltpu.VMEM((parts, rows, tile), f32),
            mask,
            mask,
            put,
            put,
            put,
            put,
            ret,
            ret,
            ret,
            ret,
            pltpu.SemaphoreType.DMA,
            pltpu.SemaphoreType.DMA((parts,)),
            pltpu.SemaphoreType.DMA((parts,)),
            sems,
            sems,
            sems,
            sems,
        ],
        compiler_params=pltpu.CompilerParams(
            collective_id=0, has_side_effects=True, vmem_limit_bytes=48 * 1024 * 1024
        ),
        cost_estimate=pl.CostEstimate(
            flops=flops, bytes_accessed=count * tile * tile * 2 + rows * width * 20, transcendentals=0
        ),
    )(table, objective, demands, multipliers, unit_kind.reshape(1, width), meta, matrix_tiles)
    return solution_x, new_w, scalars[:2], scalars[2:]


def solution(mesh):
    in_specs = (
        P(("groups", "bundle"), None),
        P(("groups", "bundle"), None),
        P(("groups", "bundle"), None),
        P(("groups", "bundle")),
        P("groups", None, None),
        P("groups"),
        P("groups"),
        P("groups"),
        P(("groups", "bundle")),
        P("groups"),
    )
    out_specs = (
        P(("groups", "bundle"), None),
        P(("groups", "bundle"), None),
        P("groups"),
        P("groups"),
    )
    return jax.shard_map(functools.partial(shards, mesh.shape["bundle"]), mesh=mesh, in_specs=in_specs, out_specs=out_specs, check_vma=False)
```

```python
import functools

import jax
import jax.numpy as jnp
from jax import lax
from jax.experimental import pallas as pl
from jax.experimental.pallas import tpu as pltpu
from jax.sharding import PartitionSpec as P

NODES2 = 8
ITERS = 2
PDHG_STEPS = 2


step_tau = 0.4
step_sigma = 0.4
penalty = 0.5


def forward(grouped_tiles, sorted_cols, vector):
    batch_size = vector.shape[0]
    con_blocks, per_row, tile_size = (
        grouped_tiles.shape[0],
        grouped_tiles.shape[1],
        grouped_tiles.shape[2],
    )
    blocks = vector.reshape(batch_size, -1, tile_size)
    picked = jnp.take(blocks, sorted_cols, axis=1).reshape(
        batch_size, con_blocks, per_row, tile_size
    )
    product = jnp.einsum(
        "rkij,srkj->sri", grouped_tiles, picked, preferred_element_type=jnp.float32
    )
    return product.reshape(batch_size, -1)


def backward(grouped_tiles, cols_onehot, vector):
    batch_size = vector.shape[0]
    con_blocks, per_row, tile_size = (
        grouped_tiles.shape[0],
        grouped_tiles.shape[1],
        grouped_tiles.shape[2],
    )
    blocks = vector.reshape(batch_size, con_blocks, tile_size)
    product = jnp.einsum(
        "rkij,sri->srkj", grouped_tiles, blocks, preferred_element_type=jnp.float32
    )
    product = product.reshape(batch_size, con_blocks * per_row, tile_size)
    summed = jnp.einsum("vt,stj->svj", cols_onehot, product, precision=lax.Precision.HIGH)
    return summed.reshape(batch_size, -1)


def general(
    objective,
    demands,
    multipliers,
    probability,
    matrix_tiles,
    tile_row,
    tile_col,
    unit_kind,
    leaf_node,
    node_parent,
):
    scen_count = objective.shape[0]
    section_width = multipliers.shape[1] // 3
    tile_size = matrix_tiles.shape[1]
    var_blocks = objective.shape[1] // tile_size
    con_blocks = demands.shape[1] // tile_size
    tile_order = jnp.argsort(tile_row, stable=True)
    grouped_tiles = jnp.take(matrix_tiles, tile_order, axis=0).reshape(
        con_blocks, -1, tile_size, tile_size
    )
    sorted_cols = jnp.take(tile_col, tile_order)
    cols_onehot = (sorted_cols[None, :] == jnp.arange(var_blocks, dtype=jnp.int32)[:, None]).astype(
        jnp.float32
    )
    upper = jnp.where(unit_kind == 1, 1.0, 3.0).astype(jnp.float32)
    member_three = (
        leaf_node[:, None] == jnp.arange(node_parent.shape[0], dtype=jnp.int32)[None, :]
    ).astype(jnp.float32)
    parent_map = (node_parent[:, None] == jnp.arange(NODES2, dtype=jnp.int32)[None, :]).astype(
        jnp.float32
    )
    member_two = jnp.dot(member_three, parent_map, precision=lax.Precision.HIGHEST)
    member_one = jnp.ones((scen_count, 1), jnp.float32)
    members = (member_one, member_two, member_three)
    local_weights = jnp.concatenate(
        [jnp.dot(probability, member, precision=lax.Precision.HIGHEST) for member in members]
    )
    node_totals = lax.psum(local_weights, "bundle")
    total_prob = node_totals[0]
    weight_flat = jnp.repeat(node_totals, section_width)
    zeros_section = jnp.zeros((scen_count, section_width), jnp.float32)

    def primal_dual(primal, dual, linear, anchor, dual_back):
        if dual_back is None:
            dual_back = backward(grouped_tiles, cols_onehot, dual.astype(jnp.bfloat16))
        gradient = linear + dual_back
        if anchor is not None:
            gradient = gradient + penalty * jnp.concatenate(
                [primal[:, : 3 * section_width] - anchor, zeros_section], axis=1
            )
        moved = jnp.clip(primal - step_tau * gradient, 0.0, upper)
        image = forward(grouped_tiles, sorted_cols, (2.0 * moved - primal).astype(jnp.bfloat16))
        return (moved, jnp.maximum(dual + step_sigma * (image - demands), 0.0))

    primal = jnp.zeros_like(objective)
    dual = jnp.zeros_like(demands)
    spoke_primal = primal
    spoke_dual = dual
    weights_now = multipliers
    anchor = None
    hub_back = None
    spoke_back = None
    gap_terms = []
    bound_terms = []
    for iteration in range(ITERS):
        linear = objective + jnp.concatenate([weights_now, zeros_section], axis=1)
        for inner in range(PDHG_STEPS):
            primal, dual = primal_dual(
                primal, dual, linear, anchor, hub_back if inner == 0 else None
            )
        hub_back = None
        pieces = []
        for section_index in range(3):
            consensus_member = members[section_index]
            part_values = primal[
                :, section_index * section_width : (section_index + 1) * section_width
            ]
            weighted = consensus_member * probability[:, None]
            pieces.append(
                jnp.dot(weighted.T, part_values, precision=lax.Precision.HIGHEST).reshape(-1)
            )
        flat_sums = jnp.concatenate(pieces)
        mean_values = lax.psum(flat_sums, "bundle") / weight_flat
        result = []
        offset = 0
        for consensus_member in members:
            node_count = consensus_member.shape[1]
            node_table = mean_values[offset : offset + node_count * section_width].reshape(
                node_count, section_width
            )
            result.append(jnp.dot(consensus_member, node_table, precision=lax.Precision.HIGHEST))
            offset = offset + node_count * section_width
        agreed = jnp.concatenate(result, axis=1)
        deviation = primal[:, : 3 * section_width] - agreed
        gap_term = jnp.sum(probability * jnp.sum(deviation * deviation, axis=1))
        if iteration == 0:
            spoke_primal, spoke_dual = (primal, dual)
        else:
            for inner in range(PDHG_STEPS):
                spoke_primal, spoke_dual = primal_dual(
                    spoke_primal, spoke_dual, linear, None, spoke_back if inner == 0 else None
                )
        spoke_back = backward(grouped_tiles, cols_onehot, spoke_dual.astype(jnp.bfloat16))
        if iteration == 0:
            hub_back = spoke_back
        reduced = linear + spoke_back
        bound_term = jnp.sum(
            probability
            * (jnp.sum(reduced * spoke_primal, axis=1) - jnp.sum(demands * spoke_dual, axis=1))
        )
        gap_terms.append(lax.psum(gap_term, "bundle"))
        bound_terms.append(lax.psum(bound_term, "bundle"))
        weights_now = weights_now + penalty * deviation
        anchor = agreed
    gap_totals = jnp.stack(gap_terms)
    bound_totals = jnp.stack(bound_terms)
    hedging_gap = gap_totals / (3 * section_width * total_prob)
    lagrange_bound = bound_totals / (objective.shape[1] * total_prob)
    return (primal, weights_now, hedging_gap, lagrange_bound)


MESH = pl.DeviceIdType.MESH
ROW_TILE, ROW_COL, COL_TILE, COL_ROW, COL_KEEP, COL_LAST = range(6)
HIGHEST = lax.Precision.HIGHEST


def tables(tile_row, tile_col, var_blocks):
    count = tile_row.shape[0]
    place = jnp.arange(count, dtype=jnp.int32)
    keys = jnp.stack([tile_row, tile_col]) * count + place
    rank = jnp.sum((keys[:, None, :] < keys[:, :, None]).astype(jnp.int32), axis=2)
    code = place + count * (tile_row + 256 * tile_col)
    hit = rank[:, :, None] == place[None, None, :]
    packed = jnp.sum(jnp.where(hit, code[None, :, None], 0), axis=1)
    tile = packed % count
    row = (packed // count) % 256
    col = packed // (count * 256)
    keep = jnp.concatenate([jnp.zeros(1, jnp.int32), (col[1, 1:] == col[1, :-1]).astype(jnp.int32)])
    block = jnp.arange(count, dtype=jnp.int32)
    upto = jnp.sum((tile_col[None, :] <= block[:, None]).astype(jnp.int32), axis=1)
    own = jnp.any(tile_col[None, :] == block[:, None], axis=1)
    last = jnp.where(own, upto - 1, count)
    return jnp.concatenate([tile[0], col[0], tile[1], row[1], keep, last])


def mega(
    parts,
    idx_ref,
    objective_ref,
    demands_ref,
    mult_ref,
    kind_ref,
    meta_ref,
    tiles_hbm,
    x_out,
    w_out,
    scalars_out,
    tiles,
    x,
    y,
    xs,
    ys,
    q,
    h,
    a,
    h2,
    a2,
    runs,
    runs2,
    meta_all,
    mask2,
    mask3,
    put1,
    got1,
    put2,
    got2,
    back1,
    ret1,
    back2,
    ret2,
    tile_sem,
    meta_send,
    meta_recv,
    put_send,
    put_recv,
    ret_send,
    ret_recv,
):
    me = lax.axis_index("bundle")
    blocks = x.shape[0]
    rows = x.shape[1]
    count = tiles.shape[0]
    con_blocks = y.shape[0]
    per_row = count // con_blocks
    free = blocks - 3 * parts

    tile_copy = pltpu.make_async_copy(tiles_hbm, tiles, tile_sem)
    tile_copy.start()

    barrier = pltpu.get_barrier_semaphore()

    def greet(k, carry):
        pl.semaphore_signal(
            barrier, inc=1, device_id={"bundle": lax.rem(me + k, parts)}, device_id_type=MESH
        )
        return carry

    lax.fori_loop(1, parts, greet, 0)

    def lanes(block):
        return pl.ds(pl.multiple_of(block * 128, 128), 128)

    def upper(block):
        return jnp.where(kind_ref[:, lanes(block)] == 1, 1.0, 3.0).astype(jnp.float32)

    def index(table, item):
        return idx_ref[table * count + item]

    def first(block, with_w):
        linear = objective_ref[:, lanes(block)]
        if with_w:
            linear = linear + mult_ref[:, lanes(block)]
        q[block] = linear
        moved = jnp.clip(-step_tau * linear, 0.0, upper(block))
        x[block] = moved
        h[block] = (2.0 * moved).astype(jnp.bfloat16)

    def loop(start, stop, width, body):
        def many(i, carry):
            for u in range(width):
                body(start + i * width + u)
            return carry

        lax.fori_loop(0, (stop - start) // width, many, 0)

    loop(0, 3 * parts, 8, lambda block: first(block, True))
    loop(3 * parts, blocks, 8, lambda block: first(block, False))

    pl.semaphore_wait(barrier, parts - 1)

    def meta_copy(k):
        return pltpu.make_async_remote_copy(
            src_ref=meta_ref,
            dst_ref=meta_all.at[me],
            send_sem=meta_send.at[k],
            recv_sem=meta_recv.at[k],
            device_id={"bundle": lax.rem(me + k, parts)},
            device_id_type=MESH,
        )

    def put_copy(k, put, got, turn):
        peer = lax.rem(me + k, parts)
        return pltpu.make_async_remote_copy(
            src_ref=put.at[peer],
            dst_ref=got.at[me],
            send_sem=put_send.at[turn, k],
            recv_sem=put_recv.at[turn, k],
            device_id={"bundle": peer},
            device_id_type=MESH,
        )

    def ret_copy(k, back, ret, turn):
        peer = lax.rem(me + k, parts)
        return pltpu.make_async_remote_copy(
            src_ref=back.at[peer],
            dst_ref=ret.at[me],
            send_sem=ret_send.at[turn, k],
            recv_sem=ret_recv.at[turn, k],
            device_id={"bundle": peer},
            device_id_type=MESH,
        )

    def each(body):
        def step(k, carry):
            body(k)
            return carry

        lax.fori_loop(1, parts, step, 0)

    each(lambda k: meta_copy(k).start())
    meta_all[me] = meta_ref[...]

    def forward(vec, done):
        def row(r):
            picked = [vec[index(ROW_COL, r * per_row + k)] for k in range(per_row)]
            mats = [tiles[index(ROW_TILE, r * per_row + k)] for k in range(per_row)]
            image = lax.dot_general(
                jnp.concatenate(picked, axis=1),
                jnp.concatenate(mats, axis=1),
                (((1,), (1,)), ((), ())),
                preferred_element_type=jnp.float32,
            )
            done(r, image)

        loop(0, con_blocks, 16, row)

    def backward(vec, into):
        into[count] = jnp.zeros(into.shape[1:], jnp.float32)

        def many(i, total):
            for u in range(32):
                t = i * 32 + u
                product = jnp.dot(
                    vec[index(COL_ROW, t)],
                    tiles[index(COL_TILE, t)],
                    preferred_element_type=jnp.float32,
                )
                total = jnp.where(index(COL_KEEP, t) == 1, total, 0.0) + product
                into[t] = total
            return total

        lax.fori_loop(0, count // 32, many, jnp.zeros(into.shape[1:], jnp.float32))

    tile_copy.wait()

    def dual_first(r, image):
        new = jnp.maximum(step_sigma * (image - demands_ref[:, lanes(r)]), 0.0)
        y[r] = new
        a[r] = new.astype(jnp.bfloat16)

    forward(h, dual_first)
    backward(a, runs)

    def second(block):
        old = x[block]
        gradient = q[block] + runs[index(COL_LAST, block)]
        moved = jnp.clip(old - step_tau * gradient, 0.0, upper(block))
        x[block] = moved
        h[block] = (2.0 * moved - old).astype(jnp.bfloat16)
        return moved

    def scatter(update, put, got, turn):
        def column(owner):
            for section in range(3):
                put[owner, section * rows : (section + 1) * rows, :] = update(
                    section * parts + owner
                )

        def send(k):
            column(lax.rem(me + k, parts))
            put_copy(k, put, got, turn).start()

        each(send)
        column(me)
        got[me] = put[me]

    scatter(second, put1, got1, 0)
    loop(3 * parts, blocks, 8, second)

    each(lambda k: meta_copy(k).wait_recv())
    table = meta_all[...].reshape(parts * rows, 128)
    across = table.T
    leaf_col, p_col, two_col = table[:, 0:1], table[:, 1:2], table[:, 2:3]
    leaf_row, p_row, two_row = across[0:1, :], across[1:2, :], across[2:3, :]
    mask3[...] = jnp.where(leaf_col == leaf_row, p_row, 0.0)
    mask2[...] = jnp.where(two_col == two_row, p_row, 0.0)

    def dual_second(r, image):
        new = jnp.maximum(y[r] + step_sigma * (image - demands_ref[:, lanes(r)]), 0.0)
        y[r] = new
        a[r] = new.astype(jnp.bfloat16)

    forward(h, dual_second)
    backward(a, runs)

    my_p = meta_ref[:, 1:2]

    def bound(primal, dual, carry_runs):
        def body(i, total):
            for u in range(8):
                block = i * 8 + u
                total = total + (
                    (q[block] + carry_runs[index(COL_LAST, block)]) * primal(block)
                    - demands_ref[:, lanes(block)] * dual(block)
                )
            return total

        total = lax.fori_loop(0, blocks // 8, body, jnp.zeros((rows, 128), jnp.float32))
        return jnp.sum(my_p * total, axis=0, keepdims=True)

    bound_first = bound(lambda block: x[block], lambda block: y[block], runs)

    def consensus(put, got, back, ret, bound_row, turn):
        each(lambda k: put_copy(k, put, got, turn).wait_recv())
        everyone = meta_all[...].reshape(parts * rows, 128)
        prob = everyone[:, 1:2]
        one, two, three = [
            got[:, section * rows : (section + 1) * rows, :].reshape(parts * rows, 128)
            for section in range(3)
        ]
        weights3, weights2 = mask3[...], mask2[...]
        mean3 = jnp.dot(weights3, three, precision=HIGHEST) / jnp.sum(
            weights3, axis=1, keepdims=True
        )
        mean2 = jnp.dot(weights2, two, precision=HIGHEST) / jnp.sum(
            weights2, axis=1, keepdims=True
        )
        mean1 = jnp.sum(prob * one, axis=0, keepdims=True) / jnp.sum(prob, keepdims=True)
        square = (three - mean3) ** 2 + (two - mean2) ** 2 + (one - mean1) ** 2
        gap_row = jnp.sum(prob * square, axis=0, keepdims=True)
        back[:, 0:rows, :] = mean3.reshape(parts, rows, 128)
        back[:, rows : 2 * rows, :] = mean2.reshape(parts, rows, 128)
        line = lax.broadcasted_iota(jnp.int32, (8, 128), 0)
        extra = jnp.where(
            line == 0, mean1, jnp.where(line == 1, gap_row, jnp.where(line == 2, bound_row, 0.0))
        )
        back[:, 2 * rows :, :] = jnp.broadcast_to(extra[None], (parts, 8, 128))
        each(lambda k: ret_copy(k, back, ret, turn).start())
        ret[me] = back[me]
        each(lambda k: ret_copy(k, back, ret, turn).wait_recv())

    def drain(put, got, back, ret, turn):
        each(lambda k: put_copy(k, put, got, turn).wait_send())
        each(lambda k: ret_copy(k, back, ret, turn).wait_send())

    def agreed(ret, section, owner):
        if section == 0:
            return ret[owner, 2 * rows : 2 * rows + 1, :]
        if section == 1:
            return ret[owner, rows : 2 * rows, :]
        return ret[owner, 0:rows, :]

    consensus(put1, got1, back1, ret1, bound_first, 0)

    def third(block, section, owner):
        old = x[block]
        linear = q[block]
        carry = runs[index(COL_LAST, block)]
        limit = upper(block)
        if section is None:
            moved = jnp.clip(old - step_tau * (linear + carry), 0.0, limit)
            spoke = moved
        else:
            mean = agreed(ret1, section, owner)
            half = penalty * (old - mean)
            w = mult_ref[:, lanes(block)] + half
            w_out[:, lanes(block)] = w
            linear = objective_ref[:, lanes(block)] + w
            q[block] = linear
            gradient = linear + carry
            moved = jnp.clip(old - step_tau * (gradient + half), 0.0, limit)
            spoke = jnp.clip(old - step_tau * gradient, 0.0, limit)
        x[block] = moved
        xs[block] = spoke
        h2[block] = jnp.concatenate(
            [2.0 * moved - old, 2.0 * spoke - old], axis=0
        ).astype(jnp.bfloat16)

    def sections(body):
        def step(owner):
            for section in range(3):
                body(section * parts + owner, section, owner)

        loop(0, parts, 4, step)

    sections(third)
    loop(3 * parts, blocks, 8, lambda block: third(block, None, None))

    def dual_third(r, image):
        old = y[r]
        right = demands_ref[:, lanes(r)]
        hub = jnp.maximum(old + step_sigma * (image[0:rows] - right), 0.0)
        spoke = jnp.maximum(old + step_sigma * (image[rows:] - right), 0.0)
        ys[r] = spoke
        a2[r] = jnp.concatenate([hub, spoke], axis=0).astype(jnp.bfloat16)

    forward(h2, dual_third)
    backward(a2, runs2)

    def fourth(block, section, owner):
        both = runs2[index(COL_LAST, block)]
        linear = q[block]
        limit = upper(block)
        old = x[block]
        gradient = linear + both[0:rows]
        if section is not None:
            gradient = gradient + penalty * (old - agreed(ret1, section, owner))
        moved = jnp.clip(old - step_tau * gradient, 0.0, limit)
        x_out[:, lanes(block)] = moved
        old_spoke = xs[block]
        spoke = jnp.clip(old_spoke - step_tau * (linear + both[rows:]), 0.0, limit)
        xs[block] = spoke
        h[block] = (2.0 * spoke - old_spoke).astype(jnp.bfloat16)
        return moved

    each(lambda k: meta_copy(k).wait_send())
    drain(put1, got1, back1, ret1, 0)

    def scatter_last():
        def column(owner):
            for section in range(3):
                put2[owner, section * rows : (section + 1) * rows, :] = fourth(
                    section * parts + owner, section, owner
                )

        def send(k):
            column(lax.rem(me + k, parts))
            put_copy(k, put2, got2, 1).start()

        each(send)
        column(me)
        got2[me] = put2[me]

    scatter_last()
    loop(3 * parts, blocks, 8, lambda block: fourth(block, None, None))

    def dual_fourth(r, image):
        new = jnp.maximum(ys[r] + step_sigma * (image - demands_ref[:, lanes(r)]), 0.0)
        ys[r] = new
        a[r] = new.astype(jnp.bfloat16)

    forward(h, dual_fourth)
    backward(a, runs)
    bound_second = bound(lambda block: xs[block], lambda block: ys[block], runs)
    consensus(put2, got2, back2, ret2, bound_second, 1)

    def finish(block, section, owner):
        w_out[:, lanes(block)] = w_out[:, lanes(block)] + penalty * (
            x_out[:, lanes(block)] - agreed(ret2, section, owner)
        )

    sections(finish)
    drain(put2, got2, back2, ret2, 1)
    total = jnp.sum(meta_all[...].reshape(parts * rows, 128)[:, 1:2])
    gap_scale = 1.0 / (3 * parts * 128 * total)
    bound_scale = 1.0 / (blocks * 128 * total)
    for iteration, ret in enumerate((ret1, ret2)):
        scalars_out[iteration] = jnp.sum(ret[:, 2 * rows + 1 : 2 * rows + 2, :]) * gap_scale
        scalars_out[2 + iteration] = jnp.sum(ret[:, 2 * rows + 2 : 2 * rows + 3, :]) * bound_scale


def shards(
    parts,
    objective,
    demands,
    multipliers,
    probability,
    matrix_tiles,
    tile_row,
    tile_col,
    unit_kind,
    leaf_node,
    node_parent,
):
    rows, width = objective.shape
    tile = matrix_tiles.shape[1]
    section = multipliers.shape[1] // 3
    count = matrix_tiles.shape[0]
    fits = (
        tile == 128
        and rows == 16
        and section == parts * tile
        and width == demands.shape[1]
        and width // tile <= min(count, 256)
        and parts > 1
    )
    if not fits:
        return general(
            objective,
            demands,
            multipliers,
            probability,
            matrix_tiles,
            tile_row,
            tile_col,
            unit_kind,
            leaf_node,
            node_parent,
        )
    blocks = width // tile
    table = tables(tile_row, tile_col, blocks)
    nodes = jnp.arange(node_parent.shape[0], dtype=jnp.int32)
    parent = jnp.sum(
        jnp.where(leaf_node[:, None] == nodes[None, :], node_parent[None, :], 0), axis=1
    )
    lane = jnp.arange(tile)[None, :]
    meta = jnp.where(
        lane == 0,
        leaf_node[:, None].astype(jnp.float32),
        jnp.where(
            lane == 1,
            probability[:, None],
            jnp.where(lane == 2, parent[:, None].astype(jnp.float32), 0.0),
        ),
    )
    f32, bf16 = jnp.float32, jnp.bfloat16
    state = pltpu.VMEM((blocks, rows, tile), f32)
    vec = pltpu.VMEM((blocks, rows, tile), bf16)
    vec2 = pltpu.VMEM((blocks, 2 * rows, tile), bf16)
    put = pltpu.VMEM((parts, 3 * rows, tile), f32)
    ret = pltpu.VMEM((parts, 2 * rows + 8, tile), f32)
    mask = pltpu.VMEM((parts * rows, parts * rows), f32)
    sems = pltpu.SemaphoreType.DMA((2, parts))
    vmem = pl.BlockSpec(memory_space=pltpu.VMEM)
    smem = pl.BlockSpec(memory_space=pltpu.SMEM)
    flops = 2 * count * tile * tile * rows * 10
    solution_x, new_w, scalars = pl.pallas_call(
        functools.partial(mega, parts),
        out_shape=(
            jax.ShapeDtypeStruct((rows, width), f32),
            jax.ShapeDtypeStruct(multipliers.shape, f32),
            jax.ShapeDtypeStruct((4,), f32),
        ),
        in_specs=[smem, vmem, vmem, vmem, vmem, vmem, pl.BlockSpec(memory_space=pl.ANY)],
        out_specs=(vmem, vmem, smem),
        scratch_shapes=[
            pltpu.VMEM(matrix_tiles.shape, bf16),
            state,
            state,
            state,
            state,
            state,
            vec,
            vec,
            vec2,
            vec2,
            pltpu.VMEM((count + 1, rows, tile), f32),
            pltpu.VMEM((count + 1, 2 * rows, tile), f32),
            pltpu.VMEM((parts, rows, tile), f32),
            mask,
            mask,
            put,
            put,
            put,
            put,
            ret,
            ret,
            ret,
            ret,
            pltpu.SemaphoreType.DMA,
            pltpu.SemaphoreType.DMA((parts,)),
            pltpu.SemaphoreType.DMA((parts,)),
            sems,
            sems,
            sems,
            sems,
        ],
        compiler_params=pltpu.CompilerParams(
            collective_id=0, has_side_effects=True, vmem_limit_bytes=48 * 1024 * 1024
        ),
        cost_estimate=pl.CostEstimate(
            flops=flops, bytes_accessed=count * tile * tile * 2 + rows * width * 20, transcendentals=0
        ),
    )(table, objective, demands, multipliers, unit_kind.reshape(1, width), meta, matrix_tiles)
    return solution_x, new_w, scalars[:2], scalars[2:]


def solution(mesh):
    in_specs = (
        P(("groups", "bundle"), None),
        P(("groups", "bundle"), None),
        P(("groups", "bundle"), None),
        P(("groups", "bundle")),
        P("groups", None, None),
        P("groups"),
        P("groups"),
        P("groups"),
        P(("groups", "bundle")),
        P("groups"),
    )
    out_specs = (
        P(("groups", "bundle"), None),
        P(("groups", "bundle"), None),
        P("groups"),
        P("groups"),
    )
    return jax.shard_map(functools.partial(shards, mesh.shape["bundle"]), mesh=mesh, in_specs=in_specs, out_specs=out_specs, check_vma=False)
```
